32 devices in a mesh: chan: 8 (over z, x), stn: 4 (over y, core).
Axes of the slice: x: 2, y: 2, z: 4, core: 2. Of those that a mesh axis runs over, the one named last changes fastest.
Arguments:
- gains: float32 [16, 2, 2, 2, 16, 512], P('chan', None, None, None, None, 'stn'), may hold values from -2.1 to 2.1
- coherency: bfloat16 [16, 16, 2, 512, 512], P('chan', None, None, 'stn'), may hold values from -1.5 to 1.5
- vis_data: bfloat16 [16, 2, 2, 2, 512, 512], P('chan', None, None, None, 'stn'), may hold values from -6 to 6
- flags: int32 [16, 32, 32], P('chan', 'stn'), may hold values 0 or 1
- beam: float32 [8, 16], replicated, may hold values from 0.5 to 2
- group_of: int32 [512], replicated, may hold values from 0 to 7
Outputs:
- gain_step: float32 [16, 2, 2, 2, 16, 512], P('chan', None, None, None, None, 'stn')
- loss_value: float32 [], replicated
The draws below stay inside these ranges and needn't reach their ends.
All inputs are finite; a program needn't handle non-finite values. No bound on the sum of `flags` on one device may be relied on, other than what follows from the above.
Results may differ from the reference program's by a relative error of at most 0.0003.
Values sent between devices are 32-bit elements; how exact they have to be, the bound alone decides.
A program may use at most 128 MiB of HBM per device.

```python
import math
import jax
import jax.numpy as jnp
from jax import lax

K = 16
BLK = 16
NGRP = 8
S = 512
F = 16
NB = 32


def touch_ends(values, key, smallest, top_value):
    shape = values.shape
    place = [jax.random.randint(jax.random.fold_in(key, axis), (), 0, shape[axis]) for axis in range(len(shape))]
    values = values.at[tuple(place)].set(smallest)
    longest = shape.index(max(shape))
    place[longest] = (place[longest] + 1) % shape[longest]
    return values.at[tuple(place)].set(top_value)


def steps_of(own_key, shape, cuts, least, largest):
    gain, own = 1.0, jax.random.fold_in(own_key, 6)
    for axis_at, shards_of in cuts:
        heights = jnp.exp(jax.random.uniform(jax.random.fold_in(own, axis_at), (shards_of,), jnp.float32, least / len(cuts), largest / len(cuts)))
        gain = gain * jnp.repeat(heights, shape[axis_at] // shards_of).reshape([-1 if axis == axis_at else 1 for axis in range(len(shape))])
    return gain


def scatter_about(own_key, shape, scale, most, split=(), held_as=jnp.bfloat16):
    level = steps_of(own_key, shape, split, -0.22, 0.18) if split else 1.0
    array = jax.random.normal(own_key, shape, jnp.float32) * scale * level
    return jnp.minimum(jnp.maximum(array, -most), most).astype(held_as)


def setup_inputs(seed: int = 0) -> dict:
    key_list = jax.random.split(jax.random.key(seed), 7)
    return {
        "gains": scatter_about(key_list[0], (F, 2, 2, 2, K, S), 0.35, 2.1, ((0, 8), (5, 4)), jnp.float32),
        "coherency": scatter_about(key_list[1], (F, K, 2, S, S), 0.25, 1.5, ((0, 8), (3, 4))),
        "vis_data": scatter_about(key_list[2], (F, 2, 2, 2, S, S), 1.0, 6.0, ((0, 8), (4, 4))),
        "flags": touch_ends((jax.random.randint(key_list[3], (F, NB, NB), 0, 4) < 3).astype(jnp.int32), jax.random.fold_in(key_list[3], 1), 0, 1),
        "beam": jnp.clip(jnp.exp(jax.random.uniform(key_list[4], (NGRP, K), jnp.float32, math.log(0.5), math.log(2.0))), 0.5, 2.0),
        "group_of": touch_ends(jax.random.randint(key_list[5], (S,), 0, NGRP), jax.random.fold_in(key_list[5], 1), 0, NGRP - 1).astype(jnp.int32),
    }


smooth_weight = 0.05
damping = 0.3


def beam_factor(beam, group_of):
    groups = beam.shape[0]
    onehot = (group_of[None, :] == jnp.arange(groups, dtype=jnp.int32)[:, None]).astype(jnp.float32)
    return jnp.sum(beam[:, :, None] * onehot[:, None, :], axis=0)


def expand_flags(flags):
    chans, first, second = flags.shape
    wide = jnp.broadcast_to(flags.astype(jnp.float32)[:, :, None, :, None], (chans, first, BLK, second, BLK))
    return wide.reshape(chans, first * BLK, second * BLK)


def outer_product(row_dir, col_dir):
    row_real = row_dir[:, 0][:, :, None, :, :, None]
    row_imag = row_dir[:, 1][:, :, None, :, :, None]
    col_real = col_dir[:, 0][:, None, :, :, None, :]
    col_imag = col_dir[:, 1][:, None, :, :, None, :]
    real_part = jnp.sum(row_real * col_real + row_imag * col_imag, axis=3)
    imag_part = jnp.sum(row_imag * col_real - row_real * col_imag, axis=3)
    return real_part, imag_part


def block_terms(coherency, vis_data, weight, row_gains, col_gains):
    count_dirs = row_gains.shape[4]
    chans, row_total, col_total = weight.shape
    empty = jnp.zeros((chans, 2, 2, row_total, col_total), jnp.float32)

    def model_turn(state_pair, dir_index):
        coh_dir = lax.dynamic_index_in_dim(coherency, dir_index, 1, False).astype(jnp.float32)
        coh_real = coh_dir[:, 0][:, None, None]
        coh_imag = coh_dir[:, 1][:, None, None]
        row_dir = lax.dynamic_index_in_dim(row_gains, dir_index, 4, False)
        col_dir = lax.dynamic_index_in_dim(col_gains, dir_index, 4, False)
        outer_real, outer_imag = outer_product(row_dir, col_dir)
        model_real = state_pair[0] + coh_real * outer_real - coh_imag * outer_imag
        model_imag = state_pair[1] + coh_real * outer_imag + coh_imag * outer_real
        return (model_real, model_imag), None

    dir_list = jnp.arange(count_dirs, dtype=jnp.int32)
    (model_real, model_imag), _ = lax.scan(model_turn, (empty, empty), dir_list)
    observed = vis_data.astype(jnp.float32)
    res_real = weight[:, None, None] * (observed[:, 0] - model_real)
    res_imag = weight[:, None, None] * (observed[:, 1] - model_imag)
    total_sq = jnp.sum(res_real * res_real + res_imag * res_imag)
    wide_real = res_real[:, :, :, None]
    wide_imag = res_imag[:, :, :, None]

    def gradient_turn(state_dummy, dir_index):
        coh_dir = lax.dynamic_index_in_dim(coherency, dir_index, 1, False).astype(jnp.float32)
        coh_real = coh_dir[:, 0][:, None, None]
        coh_imag = coh_dir[:, 1][:, None, None]
        row_dir = lax.dynamic_index_in_dim(row_gains, dir_index, 4, False)
        col_dir = lax.dynamic_index_in_dim(col_gains, dir_index, 4, False)
        col_real = col_dir[:, 0][:, None, :, :, None, :]
        col_imag = col_dir[:, 1][:, None, :, :, None, :]
        prod_real = jnp.sum(wide_real * col_real - wide_imag * col_imag, axis=2)
        prod_imag = jnp.sum(wide_real * col_imag + wide_imag * col_real, axis=2)
        row_grad_real = -jnp.sum(coh_real * prod_real + coh_imag * prod_imag, axis=-1)
        row_grad_imag = -jnp.sum(coh_real * prod_imag - coh_imag * prod_real, axis=-1)
        row_real = row_dir[:, 0][:, :, None, :, :, None]
        row_imag = row_dir[:, 1][:, :, None, :, :, None]
        herm_real = jnp.sum(wide_real * row_real + wide_imag * row_imag, axis=1)
        herm_imag = jnp.sum(wide_real * row_imag - wide_imag * row_real, axis=1)
        col_grad_real = -jnp.sum(coh_real * herm_real - coh_imag * herm_imag, axis=-2)
        col_grad_imag = -jnp.sum(coh_real * herm_imag + coh_imag * herm_real, axis=-2)
        power = weight * (coh_dir[:, 0] * coh_dir[:, 0] + coh_dir[:, 1] * coh_dir[:, 1])
        col_norm = jnp.sum(col_dir * col_dir, axis=(1, 2, 3))
        row_norm = jnp.sum(row_dir * row_dir, axis=(1, 2, 3))
        row_curv = jnp.sum(power * col_norm[:, None, :], axis=-1)
        col_curv = jnp.sum(power * row_norm[:, :, None], axis=-2)
        row_grad = jnp.stack([row_grad_real, row_grad_imag], axis=1)
        col_grad = jnp.stack([col_grad_real, col_grad_imag], axis=1)
        return state_dummy, (row_grad, row_curv, col_grad, col_curv)

    _, stacked = lax.scan(gradient_turn, jnp.float32(0.0), dir_list)
    row_grad = jnp.moveaxis(stacked[0], 0, 4)
    row_curv = jnp.moveaxis(stacked[1], 0, 1)
    col_grad = jnp.moveaxis(stacked[2], 0, 4)
    col_curv = jnp.moveaxis(stacked[3], 0, 1)
    return total_sq, row_grad, row_curv, col_grad, col_curv


def reference(gains, coherency, vis_data, flags, beam, group_of):
    factor = beam_factor(beam, group_of)
    effective = gains * factor
    station_ids = jnp.arange(S, dtype=jnp.int32)
    off_diagonal = (station_ids[:, None] != station_ids[None, :]).astype(jnp.float32)

    def per_channel(channel_items):
        coh_one, data_one, flag_one, gain_one = channel_items
        weight = expand_flags(flag_one[None]) * off_diagonal[None]
        results = block_terms(coh_one[None], data_one[None], weight, gain_one[None], gain_one[None])
        return (results[0], jnp.sum(weight), results[1][0], results[2][0], results[3][0], results[4][0])

    sq_all, count_all, row_grad, row_curv, col_grad, col_curv = lax.map(
        per_channel, (coherency, vis_data, flags, effective))
    count = jnp.sum(count_all)
    total_sq = jnp.sum(sq_all)
    norm_scale = (F * S) / count
    second = gains[2:] - 2.0 * gains[1:-1] + gains[:-2]
    pad_spec = [(1, 1)] + [(0, 0)] * 5
    diff_full = jnp.pad(second, pad_spec)
    diff_pad = jnp.pad(diff_full, pad_spec)
    smooth_grad = diff_pad[:-2] - 2.0 * diff_pad[1:-1] + diff_pad[2:]
    gradient = norm_scale * factor * (row_grad + col_grad) + smooth_weight * smooth_grad
    curvature = norm_scale * factor * factor * (row_curv + col_curv) + damping
    gain_step = gradient / curvature[:, None, None, None]
    loss_value = (norm_scale * total_sq + smooth_weight * jnp.sum(second * second)) / (F * S)
    return gain_step, loss_value
```

```python
import functools

import jax
import jax.numpy as jnp
from jax import lax
from jax.experimental import pallas as pl
from jax.experimental.pallas import tpu as pltpu
from jax.sharding import PartitionSpec as P

smooth_weight = 0.05
damping = 0.3
GROUP = 2
ROWS = 16


def split_pair(values):
    high = values.astype(jnp.bfloat16).astype(jnp.float32)
    return high, values - high


def dot_nn(left, right):
    return lax.dot_general(left, right, (((1,), (0,)), ((), ())), preferred_element_type=jnp.float32)


def dot_nt(left, right):
    return lax.dot_general(left, right, (((1,), (1,)), ((), ())), preferred_element_type=jnp.float32)


def dot_tn(left, right):
    return lax.dot_general(left, right, (((0,), (0,)), ((), ())), preferred_element_type=jnp.float32)


def turned(four):
    return jnp.concatenate([-four[2:4], four[0:2]], axis=0)


def kernel(
    coh, vis, flags, row_j, col_j,
    row_out, col_out, stat_out,
    right_s, left_s, norm_q, norm_p, weight_s, res, outer0, outer1,
    ehi0, elo0, ehi1, elo1, phi0, plo0, phi1, plo1,
):
    dirs = coh.shape[1]
    rows, cols = coh.shape[3], coh.shape[4]
    blocks_r, blocks_c = flags.shape[1], flags.shape[2]
    blk = cols // blocks_c

    def prepare(k, carry):
        xq = col_j[0, k]
        hq, lq = split_pair(xq)
        for b in range(2):
            for e in range(2):
                h, l = hq[4 * b:4 * b + 4], lq[4 * b:4 * b + 4]
                if e:
                    h, l = turned(h), turned(l)
                right_s[k, :, (2 * b + e) * cols:(2 * b + e + 1) * cols] = jnp.concatenate(
                    [h, l, h, l], axis=0).astype(jnp.bfloat16)
        xp = row_j[0, k]
        hp, lp = split_pair(xp)
        for e in range(2):
            for a in range(2):
                h, l = hp[4 * a:4 * a + 4], lp[4 * a:4 * a + 4]
                if e:
                    h, l = -turned(h), -turned(l)
                left_s[k, :, (2 * e + a) * rows:(2 * e + a + 1) * rows] = jnp.concatenate(
                    [h, h, l, l], axis=0).astype(jnp.bfloat16)
        for ref, x in ((norm_q, xq), (norm_p, xp)):
            total = jnp.sum(x * x, axis=0, keepdims=True)
            high, low = split_pair(total)
            place = lax.broadcasted_iota(jnp.int32, (16, x.shape[1]), 0)
            ref[k] = jnp.where(place == 0, high, jnp.where(place == 1, low, 0.0)).astype(jnp.bfloat16)
        return carry

    lax.fori_loop(0, dirs, prepare, 0)

    spread_c = (
        lax.broadcasted_iota(jnp.int32, (blocks_c, cols), 0)
        == lax.broadcasted_iota(jnp.int32, (blocks_c, cols), 1) // blk
    ).astype(jnp.float32)
    wide = dot_nn(flags[0].astype(jnp.float32), spread_c)
    first = lax.axis_index("stn") * rows
    count = jnp.zeros((blk, cols), jnp.float32)
    for i in range(blocks_r):
        ids = first + i * blk + lax.broadcasted_iota(jnp.int32, (blk, cols), 0)
        other = lax.broadcasted_iota(jnp.int32, (blk, cols), 1)
        w = jnp.where(ids != other, jnp.broadcast_to(wide[i:i + 1], (blk, cols)), 0.0)
        weight_s[i * blk:(i + 1) * blk, :] = w
        count = count + w
    stat_out[0, 0] = jnp.sum(count.reshape(blk // 8, 8, cols), axis=0)

    res[...] = jnp.zeros_like(res)

    def outer_of(start, outer):
        for g in range(GROUP):
            k = jnp.minimum(start + g, dirs - 1)
            left = left_s[k]
            for b in range(2):
                outer[g, :, b * cols:(b + 1) * cols] = dot_tn(
                    left, right_s[k, :, 2 * b * cols:(2 * b + 1) * cols])

    def add_model(start, outer):
        for r in range(0, rows, ROWS):
            c = [
                (coh[0, start + g, 0, r:r + ROWS, :].astype(jnp.float32),
                 coh[0, start + g, 1, r:r + ROWS, :].astype(jnp.float32))
                for g in range(GROUP)
            ]
            for a in range(2):
                for b in range(2):
                    at_r = slice(a * rows + r, a * rows + r + ROWS)
                    at_i = slice((2 + a) * rows + r, (2 + a) * rows + r + ROWS)
                    lane = slice(b * cols, (b + 1) * cols)
                    mr, mi = res[at_r, lane], res[at_i, lane]
                    for g in range(GROUP):
                        o_r, o_i = outer[g, at_r, lane], outer[g, at_i, lane]
                        cr, ci = c[g]
                        mr = mr + (cr * o_r - ci * o_i)
                        mi = mi + (cr * o_i + ci * o_r)
                    res[at_r, lane] = mr
                    res[at_i, lane] = mi

    outer_of(0, outer0)

    def model_turn(j, carry):
        at = j * (2 * GROUP)
        outer_of(at + GROUP, outer1)
        add_model(at, outer0)
        outer_of(at + 2 * GROUP, outer0)
        add_model(at + GROUP, outer1)
        return carry

    lax.fori_loop(0, dirs // (2 * GROUP), model_turn, 0)

    squares = jnp.zeros((8, cols), jnp.float32)
    for r in range(0, rows, ROWS):
        w = weight_s[r:r + ROWS, :]
        for e in range(2):
            for a in range(2):
                for b in range(2):
                    at = slice((2 * e + a) * rows + r, (2 * e + a) * rows + r + ROWS)
                    lane = slice(b * cols, (b + 1) * cols)
                    value = w * (vis[0, e, a, b, r:r + ROWS, :].astype(jnp.float32) - res[at, lane])
                    res[at, lane] = value
                    squares = squares + jnp.sum((value * value).reshape(ROWS // 8, 8, cols), axis=0)
    stat_out[0, 1] = squares

    def build(k, ehi, elo, phi, plo):
        for r in range(0, rows, ROWS):
            cr = coh[0, k, 0, r:r + ROWS, :].astype(jnp.float32)
            ci = coh[0, k, 1, r:r + ROWS, :].astype(jnp.float32)
            power = weight_s[r:r + ROWS, :] * (cr * cr + ci * ci)
            high = power.astype(jnp.bfloat16)
            phi[r:r + ROWS, :] = high
            plo[r:r + ROWS, :] = (power - high.astype(jnp.float32)).astype(jnp.bfloat16)
            for a in range(2):
                for b in range(2):
                    lane = slice(b * cols, (b + 1) * cols)
                    rr = res[a * rows + r:a * rows + r + ROWS, lane]
                    ri = res[(2 + a) * rows + r:(2 + a) * rows + r + ROWS, lane]
                    for e, value in ((0, cr * rr + ci * ri), (1, cr * ri - ci * rr)):
                        high = value.astype(jnp.bfloat16)
                        at = slice(a * rows + r, a * rows + r + ROWS)
                        to = slice((2 * b + e) * cols, (2 * b + e + 1) * cols)
                        ehi[at, to] = high
                        elo[at, to] = (value - high.astype(jnp.float32)).astype(jnp.bfloat16)

    def reduce(k, ehi, elo, phi, plo):
        right = right_s[k]
        left = left_s[k]
        row_g = dot_nt(right, ehi[...]) + dot_nt(right, elo[...])
        row_g = row_g[0:4] + row_g[4:8]
        at = pl.multiple_of(k * 8, 8)
        row_out[0, pl.ds(at, 8), :] = jnp.concatenate([row_g[:, :rows], row_g[:, rows:]], axis=0)
        parts = []
        for b in range(2):
            total = None
            for e in range(2):
                lane = slice((2 * b + e) * cols, (2 * b + e + 1) * cols)
                side = left[:, e * 2 * rows:(e + 1) * 2 * rows]
                term = dot_nn(side, ehi[:, lane]) + dot_nn(side, elo[:, lane])
                total = term if total is None else total + term
            parts.append(total[0:4] + total[8:12])
        col_out[0, pl.ds(at, 8), :] = jnp.concatenate(parts, axis=0)
        row_c = dot_nt(norm_q[k], phi[...]) + dot_nt(norm_q[k], plo[...])
        col_c = dot_nn(norm_p[k], phi[...]) + dot_nn(norm_p[k], plo[...])
        row_out[0, pl.ds(dirs * 8 + k, 1), :] = row_c[0:1] + row_c[1:2]
        col_out[0, pl.ds(dirs * 8 + k, 1), :] = col_c[0:1] + col_c[1:2]

    set0 = (ehi0, elo0, phi0, plo0)
    set1 = (ehi1, elo1, phi1, plo1)
    build(0, *set0)

    def gradient_turn(j, carry):
        reduce(2 * j, *set0)
        build(2 * j + 1, *set1)
        reduce(2 * j + 1, *set1)
        build(jnp.minimum(2 * j + 2, dirs - 1), *set0)
        return carry

    lax.fori_loop(0, dirs // 2, gradient_turn, 0)


def device_terms(coherency, vis_data, flags, row_j, col_j):
    chans, dirs, _, rows, cols = coherency.shape
    bf, f4 = jnp.bfloat16, jnp.float32

    def per_chan(shape):
        rest = len(shape) - 1
        return pl.BlockSpec((1,) + tuple(shape[1:]), lambda f: (f,) + (0,) * rest)

    outs = [
        jax.ShapeDtypeStruct((chans, dirs * 9, rows), f4),
        jax.ShapeDtypeStruct((chans, dirs * 9, cols), f4),
        jax.ShapeDtypeStruct((chans, 2, 8, cols), f4),
    ]
    ins = (coherency, vis_data, flags, row_j, col_j)
    vm = pltpu.VMEM
    return pl.pallas_call(
        kernel,
        grid=(chans,),
        in_specs=[per_chan(x.shape) for x in ins],
        out_specs=[per_chan(x.shape) for x in outs],
        out_shape=outs,
        scratch_shapes=[
            vm((dirs, 16, 4 * cols), bf),
            vm((dirs, 16, 4 * rows), bf),
            vm((dirs, 16, cols), bf),
            vm((dirs, 16, rows), bf),
            vm((rows, cols), f4),
            vm((4 * rows, 2 * cols), f4),
            vm((GROUP, 4 * rows, 2 * cols), f4),
            vm((GROUP, 4 * rows, 2 * cols), f4),
            vm((2 * rows, 4 * cols), bf),
            vm((2 * rows, 4 * cols), bf),
            vm((2 * rows, 4 * cols), bf),
            vm((2 * rows, 4 * cols), bf),
            vm((rows, cols), bf),
            vm((rows, cols), bf),
            vm((rows, cols), bf),
            vm((rows, cols), bf),
        ],
        compiler_params=pltpu.CompilerParams(vmem_limit_bytes=56 * 1024 * 1024),
    )(*ins)


def on_device(gains, coherency, vis_data, flags, beam, group_of):
    chans, dirs, rows = gains.shape[0], gains.shape[4], gains.shape[5]
    stn_count = lax.axis_size("stn")
    chan_count = lax.axis_size("chan")
    stn_index = lax.axis_index("stn")
    all_stations = rows * stn_count
    all_channels = chans * chan_count
    groups = beam.shape[0]
    own_groups = lax.dynamic_slice_in_dim(group_of, stn_index * rows, rows, 0)
    onehot = (own_groups[None, :] == jnp.arange(groups, dtype=jnp.int32)[:, None]).astype(jnp.float32)
    factor = jnp.sum(beam[:, :, None] * onehot[:, None, :], axis=0)

    own_t = jnp.transpose(gains * factor, (0, 4, 2, 1, 3, 5)).reshape(chans, dirs, 8, rows)
    all_t = lax.all_gather(own_t, "stn", axis=3, tiled=True)

    ends = chan_count - 1
    last = gains[chans - 2:]
    head = gains[:2]
    before = lax.ppermute(last, "chan", [(i, i + 1) for i in range(ends)])
    after = lax.ppermute(head, "chan", [(i + 1, i) for i in range(ends)])
    extended = jnp.concatenate([before, gains, after], axis=0)
    second = extended[2:] - 2.0 * extended[1:-1] + extended[:-2]
    first_chan = lax.axis_index("chan") * chans
    positions = first_chan - 1 + jnp.arange(chans + 2, dtype=jnp.int32)
    inside = ((positions >= 1) & (positions <= all_channels - 2)).astype(jnp.float32)
    second = second * inside[:, None, None, None, None, None]
    smooth_grad = second[:-2] - 2.0 * second[1:-1] + second[2:]
    own_second = second[1:-1]
    smooth_local = jnp.sum(own_second * own_second)

    row_out, col_out, stats = device_terms(coherency, vis_data, flags, own_t, all_t)
    summed = lax.psum_scatter(col_out, "stn", scatter_dimension=2, tiled=True) + row_out
    local = jnp.stack([jnp.sum(stats[:, 0]), jnp.sum(stats[:, 1]), smooth_local])
    count_total, sq_total, smooth_total = lax.psum(local, ("chan", "stn"))

    norm_scale = all_channels * all_stations / count_total
    grad = summed[:, :dirs * 8].reshape(chans, dirs, 2, 2, 2, rows)
    grad = -jnp.transpose(grad, (0, 3, 2, 4, 1, 5))
    curv = summed[:, dirs * 8:]
    gradient = norm_scale * factor * grad + smooth_weight * smooth_grad
    curvature = norm_scale * factor * factor * curv + damping
    gain_step = gradient / curvature[:, None, None, None]
    loss_value = (norm_scale * sq_total + smooth_weight * smooth_total) / (
        all_channels * all_stations
    )
    return (gain_step, loss_value)


def solution(mesh):
    in_specs = (
        P("chan", None, None, None, None, "stn"),
        P("chan", None, None, "stn", None),
        P("chan", None, None, None, "stn", None),
        P("chan", "stn", None),
        P(),
        P(),
    )
    out_specs = (P("chan", None, None, None, None, "stn"), P())
    return jax.shard_map(
        on_device, mesh=mesh, in_specs=in_specs, out_specs=out_specs, check_vma=False
    )
```

```python
import functools

import jax
import jax.numpy as jnp
from jax import lax
from jax.experimental import pallas as pl
from jax.experimental.pallas import tpu as pltpu
from jax.sharding import PartitionSpec as P

smooth_weight = 0.05
damping = 0.3
GROUP = 2
ROWS = 16


def split_pair(values):
    high = values.astype(jnp.bfloat16).astype(jnp.float32)
    return high, values - high


def dot_nn(left, right):
    return lax.dot_general(left, right, (((1,), (0,)), ((), ())), preferred_element_type=jnp.float32)


def dot_nt(left, right):
    return lax.dot_general(left, right, (((1,), (1,)), ((), ())), preferred_element_type=jnp.float32)


def dot_tn(left, right):
    return lax.dot_general(left, right, (((0,), (0,)), ((), ())), preferred_element_type=jnp.float32)


def turned(four):
    return jnp.concatenate([-four[2:4], four[0:2]], axis=0)


def kernel(
    coh, vis, flags, col_j,
    row_out, col_out, stat_out,
    right_s, left_s, norm_q, norm_p, weight_s, res, outer0, outer1,
    ehi0, elo0, ehi1, elo1, phi0, plo0, phi1, plo1,
):
    dirs = coh.shape[1]
    rows, cols = coh.shape[3], coh.shape[4]
    blocks_r, blocks_c = flags.shape[1], flags.shape[2]
    blk = cols // blocks_c
    first = pl.multiple_of(lax.axis_index("stn") * rows, 128)

    def prepare(k, carry):
        xq = col_j[0, k]
        hq, lq = split_pair(xq)
        for b in range(2):
            for e in range(2):
                h, l = hq[4 * b:4 * b + 4], lq[4 * b:4 * b + 4]
                if e:
                    h, l = turned(h), turned(l)
                right_s[k, :, (2 * b + e) * cols:(2 * b + e + 1) * cols] = jnp.concatenate(
                    [h, l, h, l], axis=0).astype(jnp.bfloat16)
        xp = col_j[0, k, :, pl.ds(first, rows)]
        hp, lp = split_pair(xp)
        for e in range(2):
            for a in range(2):
                h, l = hp[4 * a:4 * a + 4], lp[4 * a:4 * a + 4]
                if e:
                    h, l = -turned(h), -turned(l)
                left_s[k, :, (2 * e + a) * rows:(2 * e + a + 1) * rows] = jnp.concatenate(
                    [h, h, l, l], axis=0).astype(jnp.bfloat16)
        for ref, x in ((norm_q, xq), (norm_p, xp)):
            total = jnp.sum(x * x, axis=0, keepdims=True)
            high, low = split_pair(total)
            place = lax.broadcasted_iota(jnp.int32, (16, x.shape[1]), 0)
            ref[k] = jnp.where(place == 0, high, jnp.where(place == 1, low, 0.0)).astype(jnp.bfloat16)
        return carry

    lax.fori_loop(0, dirs, prepare, 0)

    spread_c = (
        lax.broadcasted_iota(jnp.int32, (blocks_c, cols), 0)
        == lax.broadcasted_iota(jnp.int32, (blocks_c, cols), 1) // blk
    ).astype(jnp.float32)
    wide = dot_nn(flags[0].astype(jnp.float32), spread_c)
    count = jnp.zeros((blk, cols), jnp.float32)
    for i in range(blocks_r):
        ids = first + i * blk + lax.broadcasted_iota(jnp.int32, (blk, cols), 0)
        other = lax.broadcasted_iota(jnp.int32, (blk, cols), 1)
        w = jnp.where(ids != other, jnp.broadcast_to(wide[i:i + 1], (blk, cols)), 0.0)
        weight_s[i * blk:(i + 1) * blk, :] = w
        count = count + w
    stat_out[0, 0] = jnp.sum(count.reshape(blk // 8, 8, cols), axis=0)

    res[...] = jnp.zeros_like(res)

    def outer_of(start, outer):
        for g in range(GROUP):
            k = jnp.minimum(start + g, dirs - 1)
            left = left_s[k]
            for b in range(2):
                outer[g, :, b * cols:(b + 1) * cols] = dot_tn(
                    left, right_s[k, :, 2 * b * cols:(2 * b + 1) * cols])

    def add_model(start, outer):
        for r in range(0, rows, ROWS):
            c = [
                (coh[0, start + g, 0, r:r + ROWS, :].astype(jnp.float32),
                 coh[0, start + g, 1, r:r + ROWS, :].astype(jnp.float32))
                for g in range(GROUP)
            ]
            for a in range(2):
                for b in range(2):
                    at_r = slice(a * rows + r, a * rows + r + ROWS)
                    at_i = slice((2 + a) * rows + r, (2 + a) * rows + r + ROWS)
                    lane = slice(b * cols, (b + 1) * cols)
                    mr, mi = res[at_r, lane], res[at_i, lane]
                    for g in range(GROUP):
                        o_r, o_i = outer[g, at_r, lane], outer[g, at_i, lane]
                        cr, ci = c[g]
                        mr = mr + (cr * o_r - ci * o_i)
                        mi = mi + (cr * o_i + ci * o_r)
                    res[at_r, lane] = mr
                    res[at_i, lane] = mi

    outer_of(0, outer0)

    def model_turn(j, carry):
        at = j * (2 * GROUP)
        outer_of(at + GROUP, outer1)
        add_model(at, outer0)
        outer_of(at + 2 * GROUP, outer0)
        add_model(at + GROUP, outer1)
        return carry

    lax.fori_loop(0, dirs // (2 * GROUP), model_turn, 0)

    squares = jnp.zeros((8, cols), jnp.float32)
    for r in range(0, rows, ROWS):
        w = weight_s[r:r + ROWS, :]
        for e in range(2):
            for a in range(2):
                for b in range(2):
                    at = slice((2 * e + a) * rows + r, (2 * e + a) * rows + r + ROWS)
                    lane = slice(b * cols, (b + 1) * cols)
                    value = w * (vis[0, e, a, b, r:r + ROWS, :].astype(jnp.float32) - res[at, lane])
                    res[at, lane] = value
                    squares = squares + jnp.sum((value * value).reshape(ROWS // 8, 8, cols), axis=0)
    stat_out[0, 1] = squares

    def build(k, ehi, elo, phi, plo):
        for r in range(0, rows, ROWS):
            cr = coh[0, k, 0, r:r + ROWS, :].astype(jnp.float32)
            ci = coh[0, k, 1, r:r + ROWS, :].astype(jnp.float32)
            power = weight_s[r:r + ROWS, :] * (cr * cr + ci * ci)
            high = power.astype(jnp.bfloat16)
            phi[r:r + ROWS, :] = high
            plo[r:r + ROWS, :] = (power - high.astype(jnp.float32)).astype(jnp.bfloat16)
            for a in range(2):
                for b in range(2):
                    lane = slice(b * cols, (b + 1) * cols)
                    rr = res[a * rows + r:a * rows + r + ROWS, lane]
                    ri = res[(2 + a) * rows + r:(2 + a) * rows + r + ROWS, lane]
                    for e, value in ((0, cr * rr + ci * ri), (1, cr * ri - ci * rr)):
                        high = value.astype(jnp.bfloat16)
                        at = slice(a * rows + r, a * rows + r + ROWS)
                        to = slice((2 * b + e) * cols, (2 * b + e + 1) * cols)
                        ehi[at, to] = high
                        elo[at, to] = (value - high.astype(jnp.float32)).astype(jnp.bfloat16)

    def reduce(k, ehi, elo, phi, plo):
        right = right_s[k]
        left = left_s[k]
        row_g = dot_nt(right, ehi[...]) + dot_nt(right, elo[...])
        row_g = row_g[0:4] + row_g[4:8]
        at = pl.multiple_of(k * 8, 8)
        row_out[0, pl.ds(at, 8), :] = jnp.concatenate([row_g[:, :rows], row_g[:, rows:]], axis=0)
        parts = []
        for b in range(2):
            total = None
            for e in range(2):
                lane = slice((2 * b + e) * cols, (2 * b + e + 1) * cols)
                side = left[:, e * 2 * rows:(e + 1) * 2 * rows]
                term = dot_nn(side, ehi[:, lane]) + dot_nn(side, elo[:, lane])
                total = term if total is None else total + term
            parts.append(total[0:4] + total[8:12])
        col_out[0, pl.ds(at, 8), :] = jnp.concatenate(parts, axis=0)
        row_c = dot_nt(norm_q[k], phi[...]) + dot_nt(norm_q[k], plo[...])
        col_c = dot_nn(norm_p[k], phi[...]) + dot_nn(norm_p[k], plo[...])
        row_out[0, pl.ds(dirs * 8 + k, 1), :] = row_c[0:1] + row_c[1:2]
        col_out[0, pl.ds(dirs * 8 + k, 1), :] = col_c[0:1] + col_c[1:2]

    set0 = (ehi0, elo0, phi0, plo0)
    set1 = (ehi1, elo1, phi1, plo1)
    build(0, *set0)

    def gradient_turn(j, carry):
        reduce(2 * j, *set0)
        build(2 * j + 1, *set1)
        reduce(2 * j + 1, *set1)
        build(jnp.minimum(2 * j + 2, dirs - 1), *set0)
        return carry

    lax.fori_loop(0, dirs // 2, gradient_turn, 0)


def device_terms(coherency, vis_data, flags, col_j):
    chans, dirs, _, rows, cols = coherency.shape
    bf, f4 = jnp.bfloat16, jnp.float32

    def per_chan(shape):
        rest = len(shape) - 1
        return pl.BlockSpec((1,) + tuple(shape[1:]), lambda f: (f,) + (0,) * rest)

    outs = [
        jax.ShapeDtypeStruct((chans, dirs * 9, rows), f4),
        jax.ShapeDtypeStruct((chans, dirs * 9, cols), f4),
        jax.ShapeDtypeStruct((chans, 2, 8, cols), f4),
    ]
    ins = (coherency, vis_data, flags, col_j)
    vm = pltpu.VMEM
    return pl.pallas_call(
        kernel,
        grid=(chans,),
        in_specs=[per_chan(x.shape) for x in ins],
        out_specs=[per_chan(x.shape) for x in outs],
        out_shape=outs,
        scratch_shapes=[
            vm((dirs, 16, 4 * cols), bf),
            vm((dirs, 16, 4 * rows), bf),
            vm((dirs, 16, cols), bf),
            vm((dirs, 16, rows), bf),
            vm((rows, cols), f4),
            vm((4 * rows, 2 * cols), f4),
            vm((GROUP, 4 * rows, 2 * cols), f4),
            vm((GROUP, 4 * rows, 2 * cols), f4),
            vm((2 * rows, 4 * cols), bf),
            vm((2 * rows, 4 * cols), bf),
            vm((2 * rows, 4 * cols), bf),
            vm((2 * rows, 4 * cols), bf),
            vm((rows, cols), bf),
            vm((rows, cols), bf),
            vm((rows, cols), bf),
            vm((rows, cols), bf),
        ],
        compiler_params=pltpu.CompilerParams(vmem_limit_bytes=56 * 1024 * 1024),
    )(*ins)


MESH = pl.DeviceIdType.MESH


def meet(axes):
    barrier = pltpu.get_barrier_semaphore()
    total = 0
    for axis, size in axes:
        me = lax.axis_index(axis)
        for j in range(1, size):
            pl.semaphore_signal(
                barrier, inc=1, device_id={axis: lax.rem(me + j, size)}, device_id_type=MESH)
            total += 1
    pl.semaphore_wait(barrier, total)


def remote(src, dst, send, recv, axis, target):
    return pltpu.make_async_remote_copy(
        src_ref=src, dst_ref=dst, send_sem=send, recv_sem=recv,
        device_id={axis: target}, device_id_type=MESH)


def gather_kernel(
    stn_count, chan_count, gains, beam, group_of,
    all_j, factor_out, smooth_out, square_out,
    before, after, send_sem, recv_sem, side_send, side_recv,
):
    chans, dirs, rows = gains.shape[0], gains.shape[4], gains.shape[5]
    groups = beam.shape[0]
    me = lax.axis_index("stn")
    chan = lax.axis_index("chan")
    barrier = pltpu.get_barrier_semaphore()
    for j in range(1, stn_count):
        pl.semaphore_signal(
            barrier, inc=1, device_id={"stn": lax.rem(me + j, stn_count)}, device_id_type=MESH)
    up = lax.rem(chan + 1, chan_count)
    down = lax.rem(chan + chan_count - 1, chan_count)
    for target in (up, down):
        pl.semaphore_signal(barrier, inc=1, device_id={"chan": target}, device_id_type=MESH)

    first = pl.multiple_of(me * rows, 128)
    own_groups = group_of[:, pl.ds(first, rows)]
    onehot = (
        jnp.broadcast_to(own_groups, (groups, rows))
        == lax.broadcasted_iota(jnp.int32, (groups, rows), 0)
    ).astype(jnp.float32)
    high, rest = split_pair(beam[...])
    mid, low = split_pair(rest)
    factor = dot_tn(high, onehot) + (dot_tn(mid, onehot) + dot_tn(low, onehot))
    factor_out[...] = factor
    for f in range(chans):
        for e in range(2):
            for x in range(2):
                for d in range(2):
                    all_j[f, :, 4 * x + 2 * e + d, pl.ds(first, rows)] = gains[f, e, x, d] * factor

    pl.semaphore_wait(barrier, stn_count + 1)
    own = all_j.at[:, :, :, pl.ds(first, rows)]
    copies = [
        remote(own, own, send_sem.at[j - 1], recv_sem.at[j - 1], "stn", lax.rem(me + j, stn_count))
        for j in range(1, stn_count)
    ]
    sides = [
        remote(gains.at[pl.ds(chans - 2, 2)], before, side_send.at[0], side_recv.at[0], "chan", up),
        remote(gains.at[pl.ds(0, 2)], after, side_send.at[1], side_recv.at[1], "chan", down),
    ]
    for copy in copies + sides:
        copy.start()
    for copy in sides:
        copy.wait()

    last_chan = chans * chan_count - 2
    square = jnp.zeros((dirs, rows), jnp.float32)
    for e in range(2):
        for x in range(2):
            for d in range(2):
                line = (
                    [before[i, e, x, d] for i in range(2)]
                    + [gains[i, e, x, d] for i in range(chans)]
                    + [after[i, e, x, d] for i in range(2)]
                )
                second = []
                for i in range(chans + 2):
                    place = chan * chans - 1 + i
                    inside = ((place >= 1) & (place <= last_chan)).astype(jnp.float32)
                    second.append((line[i + 2] - 2.0 * line[i + 1] + line[i]) * inside)
                for i in range(chans):
                    smooth_out[i, e, x, d] = second[i] - 2.0 * second[i + 1] + second[i + 2]
                    square = square + second[i + 1] * second[i + 1]
    square_out[...] = jnp.sum(square.reshape(dirs // 8, 8, rows), axis=0)
    for copy in copies:
        copy.wait()


def finish_kernel(
    stn_count, chan_count, row_g, col_g, stats, smooth, square, factor,
    step_out, loss_out,
    landed, total, own_sums, buf_stn, buf_chan,
    send_sem, recv_sem, send_stn, recv_stn, send_chan, recv_chan,
):
    chans, _, rows = row_g.shape
    dirs = factor.shape[0]
    me, chan = lax.axis_index("stn"), lax.axis_index("chan")
    own_sums[...] = jnp.zeros_like(own_sums)
    for i in range(2):
        part = stats[0, i]
        for f in range(1, chans):
            part = part + stats[f, i]
        part = jnp.sum(part, axis=0, keepdims=True)
        line = part[:, :128]
        for at in range(128, part.shape[1], 128):
            line = line + part[:, at:at + 128]
        own_sums[i:i + 1, :] = line
    line = jnp.sum(square[...], axis=0, keepdims=True)
    part = line[:, :128]
    for at in range(128, line.shape[1], 128):
        part = part + line[:, at:at + 128]
    own_sums[2:3, :] = part
    buf_stn[me] = own_sums[...]

    meet((("stn", stn_count), ("chan", chan_count)))
    copies = []
    small = []
    for j in range(1, stn_count):
        peer = lax.rem(me + j, stn_count)
        small.append(remote(own_sums, buf_stn.at[me], send_stn.at[j - 1], recv_stn.at[j - 1], "stn", peer))
        copies.append(remote(
            col_g.at[:, :, pl.ds(pl.multiple_of(peer * rows, 128), rows)],
            landed.at[j - 1], send_sem.at[j - 1], recv_sem.at[j - 1], "stn", peer))
    for copy in small + copies:
        copy.start()
    for copy in small:
        copy.wait()
    sums = buf_stn[0]
    for i in range(1, stn_count):
        sums = sums + buf_stn[i]
    own_sums[...] = sums
    buf_chan[chan] = sums
    small = [
        remote(own_sums, buf_chan.at[chan], send_chan.at[j - 1], recv_chan.at[j - 1], "chan",
               lax.rem(chan + j, chan_count))
        for j in range(1, chan_count)
    ]
    for copy in small:
        copy.start()
    for f in range(chans):
        total[f] = row_g[f] + col_g[f, :, pl.ds(pl.multiple_of(me * rows, 128), rows)]
    for j, copy in enumerate(copies):
        copy.wait()
        for f in range(chans):
            total[f] = total[f] + landed[j, f]
    for copy in small:
        copy.wait()
    sums = buf_chan[0]
    for i in range(1, chan_count):
        sums = sums + buf_chan[i]
    sums = jnp.sum(sums, axis=1, keepdims=True)
    scale = (chans * chan_count * rows * stn_count) / sums[0:1]
    wide = jnp.broadcast_to(scale, (dirs, rows))
    gain = factor[...]
    for f in range(chans):
        curv = wide * gain * gain * total[f, dirs * 8:dirs * 9, :] + damping
        for e in range(2):
            for x in range(2):
                for d in range(2):
                    grad = total[f, pl.ds(4 * x + 2 * e + d, dirs, stride=8), :]
                    top = smooth_weight * smooth[f, e, x, d] - wide * gain * grad
                    step_out[f, e, x, d] = top / curv
    loss = (scale * sums[1:2] + smooth_weight * sums[2:3]) / (chans * chan_count * rows * stn_count)
    loss_out[...] = jnp.broadcast_to(loss, loss_out.shape)


def on_device(gains, coherency, vis_data, flags, beam, group_of):
    chans, dirs, rows = gains.shape[0], gains.shape[4], gains.shape[5]
    stn, chan = lax.axis_size("stn"), lax.axis_size("chan")
    f4 = jnp.float32
    dma, vm = pltpu.SemaphoreType.DMA, pltpu.VMEM
    shape = jax.ShapeDtypeStruct
    all_j, factor, smooth, square = pl.pallas_call(
        functools.partial(gather_kernel, stn, chan),
        out_shape=[
            shape((chans, dirs, 8, rows * stn), f4),
            shape((dirs, rows), f4),
            shape(gains.shape, f4),
            shape((8, rows), f4),
        ],
        scratch_shapes=[
            vm((2,) + gains.shape[1:], f4),
            vm((2,) + gains.shape[1:], f4),
            dma((stn - 1,)), dma((stn - 1,)), dma((2,)), dma((2,)),
        ],
        compiler_params=pltpu.CompilerParams(collective_id=0, has_side_effects=True),
    )(gains, beam, group_of.reshape(1, -1))
    row_g, col_g, stats = device_terms(coherency, vis_data, flags, all_j)
    gain_step, loss = pl.pallas_call(
        functools.partial(finish_kernel, stn, chan),
        out_shape=[shape(gains.shape, f4), shape((8, 128), f4)],
        scratch_shapes=[
            vm((stn - 1,) + row_g.shape, f4),
            vm(row_g.shape, f4),
            vm((8, 128), f4),
            vm((stn, 8, 128), f4),
            vm((chan, 8, 128), f4),
            dma((stn - 1,)), dma((stn - 1,)), dma((stn - 1,)), dma((stn - 1,)),
            dma((chan - 1,)), dma((chan - 1,)),
        ],
        compiler_params=pltpu.CompilerParams(collective_id=1, has_side_effects=True),
    )(row_g, col_g, stats, smooth, square, factor)
    return (gain_step, loss[0, 0])


def solution(mesh):
    in_specs = (
        P("chan", None, None, None, None, "stn"),
        P("chan", None, None, "stn", None),
        P("chan", None, None, None, "stn", None),
        P("chan", "stn", None),
        P(),
        P(),
    )
    out_specs = (P("chan", None, None, None, None, "stn"), P())
    return jax.shard_map(
        on_device, mesh=mesh, in_specs=in_specs, out_specs=out_specs, check_vma=False
    )
```

```python
import functools

import jax
import jax.numpy as jnp
from jax import lax
from jax.experimental import pallas as pl
from jax.experimental.pallas import tpu as pltpu
from jax.sharding import PartitionSpec as P

smooth_weight = 0.05
damping = 0.3
GROUP = 2
ROWS = 16


def split_pair(values):
    high = values.astype(jnp.bfloat16).astype(jnp.float32)
    return high, values - high


def dot_nn(left, right):
    return lax.dot_general(left, right, (((1,), (0,)), ((), ())), preferred_element_type=jnp.float32)


def dot_nt(left, right):
    return lax.dot_general(left, right, (((1,), (1,)), ((), ())), preferred_element_type=jnp.float32)


def dot_tn(left, right):
    return lax.dot_general(left, right, (((0,), (0,)), ((), ())), preferred_element_type=jnp.float32)


def turned(four):
    return jnp.concatenate([-four[2:4], four[0:2]], axis=0)


def kernel(
    coh, vis, flags, col_j,
    row_out, col_out, stat_out,
    right_s, left_s, norm_q, norm_p, weight_s, res, outer0, outer1,
    ehi0, elo0, ehi1, elo1, phi0, plo0, phi1, plo1,
):
    dirs = coh.shape[1]
    rows, cols = coh.shape[3], coh.shape[4]
    blocks_r, blocks_c = flags.shape[1], flags.shape[2]
    blk = cols // blocks_c
    first = pl.multiple_of(lax.axis_index("stn") * rows, 128)

    def prepare(k, carry):
        xq = col_j[0, k]
        hq, lq = split_pair(xq)
        for b in range(2):
            for e in range(2):
                h, l = hq[4 * b:4 * b + 4], lq[4 * b:4 * b + 4]
                if e:
                    h, l = turned(h), turned(l)
                right_s[k, :, (2 * b + e) * cols:(2 * b + e + 1) * cols] = jnp.concatenate(
                    [h, l, h, l], axis=0).astype(jnp.bfloat16)
        xp = col_j[0, k, :, pl.ds(first, rows)]
        hp, lp = split_pair(xp)
        for e in range(2):
            for a in range(2):
                h, l = hp[4 * a:4 * a + 4], lp[4 * a:4 * a + 4]
                if e:
                    h, l = -turned(h), -turned(l)
                left_s[k, :, (2 * e + a) * rows:(2 * e + a + 1) * rows] = jnp.concatenate(
                    [h, h, l, l], axis=0).astype(jnp.bfloat16)
        for ref, x in ((norm_q, xq), (norm_p, xp)):
            total = jnp.sum(x * x, axis=0, keepdims=True)
            high, low = split_pair(total)
            place = lax.broadcasted_iota(jnp.int32, (16, x.shape[1]), 0)
            ref[k] = jnp.where(place == 0, high, jnp.where(place == 1, low, 0.0)).astype(jnp.bfloat16)
        return carry

    lax.fori_loop(0, dirs, prepare, 0)

    spread_c = (
        lax.broadcasted_iota(jnp.int32, (blocks_c, cols), 0)
        == lax.broadcasted_iota(jnp.int32, (blocks_c, cols), 1) // blk
    ).astype(jnp.float32)
    wide = dot_nn(flags[0].astype(jnp.float32), spread_c)
    count = jnp.zeros((blk, cols), jnp.float32)
    for i in range(blocks_r):
        ids = first + i * blk + lax.broadcasted_iota(jnp.int32, (blk, cols), 0)
        other = lax.broadcasted_iota(jnp.int32, (blk, cols), 1)
        w = jnp.where(ids != other, jnp.broadcast_to(wide[i:i + 1], (blk, cols)), 0.0)
        weight_s[i * blk:(i + 1) * blk, :] = w
        count = count + w
    stat_out[0, 0] = jnp.sum(count.reshape(blk // 8, 8, cols), axis=0)

    res[...] = jnp.zeros_like(res)

    def outer_of(start, outer):
        for g in range(GROUP):
            k = jnp.minimum(start + g, dirs - 1)
            left = left_s[k]
            for b in range(2):
                outer[g, :, b * cols:(b + 1) * cols] = dot_tn(
                    left, right_s[k, :, 2 * b * cols:(2 * b + 1) * cols])

    def add_model(start, outer):
        for r in range(0, rows, ROWS):
            c = [
                (coh[0, start + g, 0, r:r + ROWS, :].astype(jnp.float32),
                 coh[0, start + g, 1, r:r + ROWS, :].astype(jnp.float32))
                for g in range(GROUP)
            ]
            for a in range(2):
                for b in range(2):
                    at_r = slice(a * rows + r, a * rows + r + ROWS)
                    at_i = slice((2 + a) * rows + r, (2 + a) * rows + r + ROWS)
                    lane = slice(b * cols, (b + 1) * cols)
                    mr, mi = res[at_r, lane], res[at_i, lane]
                    for g in range(GROUP):
                        o_r, o_i = outer[g, at_r, lane], outer[g, at_i, lane]
                        cr, ci = c[g]
                        mr = mr + (cr * o_r - ci * o_i)
                        mi = mi + (cr * o_i + ci * o_r)
                    res[at_r, lane] = mr
                    res[at_i, lane] = mi

    outer_of(0, outer0)

    def model_turn(j, carry):
        at = j * (2 * GROUP)
        outer_of(at + GROUP, outer1)
        add_model(at, outer0)
        outer_of(at + 2 * GROUP, outer0)
        add_model(at + GROUP, outer1)
        return carry

    lax.fori_loop(0, dirs // (2 * GROUP), model_turn, 0)

    squares = jnp.zeros((8, cols), jnp.float32)
    for r in range(0, rows, ROWS):
        w = weight_s[r:r + ROWS, :]
        for e in range(2):
            for a in range(2):
                for b in range(2):
                    at = slice((2 * e + a) * rows + r, (2 * e + a) * rows + r + ROWS)
                    lane = slice(b * cols, (b + 1) * cols)
                    value = w * (vis[0, e, a, b, r:r + ROWS, :].astype(jnp.float32) - res[at, lane])
                    res[at, lane] = value
                    squares = squares + jnp.sum((value * value).reshape(ROWS // 8, 8, cols), axis=0)
    stat_out[0, 1] = squares

    def build(k, ehi, elo, phi, plo):
        for r in range(0, rows, ROWS):
            cr = coh[0, k, 0, r:r + ROWS, :].astype(jnp.float32)
            ci = coh[0, k, 1, r:r + ROWS, :].astype(jnp.float32)
            power = weight_s[r:r + ROWS, :] * (cr * cr + ci * ci)
            high = power.astype(jnp.bfloat16)
            phi[r:r + ROWS, :] = high
            plo[r:r + ROWS, :] = (power - high.astype(jnp.float32)).astype(jnp.bfloat16)
            for a in range(2):
                for b in range(2):
                    lane = slice(b * cols, (b + 1) * cols)
                    rr = res[a * rows + r:a * rows + r + ROWS, lane]
                    ri = res[(2 + a) * rows + r:(2 + a) * rows + r + ROWS, lane]
                    for e, value in ((0, cr * rr + ci * ri), (1, cr * ri - ci * rr)):
                        high = value.astype(jnp.bfloat16)
                        at = slice(a * rows + r, a * rows + r + ROWS)
                        to = slice((2 * b + e) * cols, (2 * b + e + 1) * cols)
                        ehi[at, to] = high
                        elo[at, to] = (value - high.astype(jnp.float32)).astype(jnp.bfloat16)

    def reduce(k, ehi, elo, phi, plo):
        right = right_s[k]
        left = left_s[k]
        row_g = dot_nt(right, ehi[...]) + dot_nt(right, elo[...])
        row_g = row_g[0:4] + row_g[4:8]
        at = pl.multiple_of(k * 8, 8)
        row_out[0, pl.ds(at, 8), :] = jnp.concatenate([row_g[:, :rows], row_g[:, rows:]], axis=0)
        parts = []
        for b in range(2):
            total = None
            for e in range(2):
                lane = slice((2 * b + e) * cols, (2 * b + e + 1) * cols)
                side = left[:, e * 2 * rows:(e + 1) * 2 * rows]
                term = dot_nn(side, ehi[:, lane]) + dot_nn(side, elo[:, lane])
                total = term if total is None else total + term
            parts.append(total[0:4] + total[8:12])
        col_out[0, pl.ds(at, 8), :] = jnp.concatenate(parts, axis=0)
        row_c = dot_nt(norm_q[k], phi[...]) + dot_nt(norm_q[k], plo[...])
        col_c = dot_nn(norm_p[k], phi[...]) + dot_nn(norm_p[k], plo[...])
        row_out[0, pl.ds(dirs * 8 + k, 1), :] = row_c[0:1] + row_c[1:2]
        col_out[0, pl.ds(dirs * 8 + k, 1), :] = col_c[0:1] + col_c[1:2]

    set0 = (ehi0, elo0, phi0, plo0)
    set1 = (ehi1, elo1, phi1, plo1)
    build(0, *set0)

    def gradient_turn(j, carry):
        reduce(2 * j, *set0)
        build(2 * j + 1, *set1)
        reduce(2 * j + 1, *set1)
        build(jnp.minimum(2 * j + 2, dirs - 1), *set0)
        return carry

    lax.fori_loop(0, dirs // 2, gradient_turn, 0)


def device_terms(coherency, vis_data, flags, col_j):
    chans, dirs, _, rows, cols = coherency.shape
    bf, f4 = jnp.bfloat16, jnp.float32

    def per_chan(shape):
        rest = len(shape) - 1
        return pl.BlockSpec((1,) + tuple(shape[1:]), lambda f: (f,) + (0,) * rest)

    outs = [
        jax.ShapeDtypeStruct((chans, dirs * 9, rows), f4),
        jax.ShapeDtypeStruct((chans, dirs * 9, cols), f4),
        jax.ShapeDtypeStruct((chans, 2, 8, cols), f4),
    ]
    ins = (coherency, vis_data, flags, col_j)
    vm = pltpu.VMEM
    return pl.pallas_call(
        kernel,
        grid=(chans,),
        in_specs=[per_chan(x.shape) for x in ins],
        out_specs=[per_chan(x.shape) for x in outs],
        out_shape=outs,
        scratch_shapes=[
            vm((dirs, 16, 4 * cols), bf),
            vm((dirs, 16, 4 * rows), bf),
            vm((dirs, 16, cols), bf),
            vm((dirs, 16, rows), bf),
            vm((rows, cols), f4),
            vm((4 * rows, 2 * cols), f4),
            vm((GROUP, 4 * rows, 2 * cols), f4),
            vm((GROUP, 4 * rows, 2 * cols), f4),
            vm((2 * rows, 4 * cols), bf),
            vm((2 * rows, 4 * cols), bf),
            vm((2 * rows, 4 * cols), bf),
            vm((2 * rows, 4 * cols), bf),
            vm((rows, cols), bf),
            vm((rows, cols), bf),
            vm((rows, cols), bf),
            vm((rows, cols), bf),
        ],
        compiler_params=pltpu.CompilerParams(vmem_limit_bytes=56 * 1024 * 1024),
    )(*ins)


MESH = pl.DeviceIdType.MESH


def meet(axes):
    barrier = pltpu.get_barrier_semaphore()
    total = 0
    for axis, size in axes:
        me = lax.axis_index(axis)
        for j in range(1, size):
            pl.semaphore_signal(
                barrier, inc=1, device_id={axis: lax.rem(me + j, size)}, device_id_type=MESH)
            total += 1
    pl.semaphore_wait(barrier, total)


def remote(src, dst, send, recv, axis, target):
    return pltpu.make_async_remote_copy(
        src_ref=src, dst_ref=dst, send_sem=send, recv_sem=recv,
        device_id={axis: target}, device_id_type=MESH)


def gather_kernel(
    stn_count, chan_count, gains, beam, group_of,
    all_j, factor_out, smooth_out, square_out,
    before, after, send_sem, recv_sem, side_send, side_recv,
):
    chans, dirs, rows = gains.shape[0], gains.shape[4], gains.shape[5]
    groups = beam.shape[0]
    me = lax.axis_index("stn")
    chan = lax.axis_index("chan")
    barrier = pltpu.get_barrier_semaphore()
    for j in range(1, stn_count):
        pl.semaphore_signal(
            barrier, inc=1, device_id={"stn": lax.rem(me + j, stn_count)}, device_id_type=MESH)
    up = lax.rem(chan + 1, chan_count)
    down = lax.rem(chan + chan_count - 1, chan_count)
    for target in (up, down):
        pl.semaphore_signal(barrier, inc=1, device_id={"chan": target}, device_id_type=MESH)

    first = pl.multiple_of(me * rows, 128)
    own_groups = group_of[:, pl.ds(first, rows)]
    onehot = (
        jnp.broadcast_to(own_groups, (groups, rows))
        == lax.broadcasted_iota(jnp.int32, (groups, rows), 0)
    ).astype(jnp.float32)
    high, rest = split_pair(beam[...])
    mid, low = split_pair(rest)
    factor = dot_tn(high, onehot) + (dot_tn(mid, onehot) + dot_tn(low, onehot))
    factor_out[...] = factor
    for f in range(chans):
        for e in range(2):
            for x in range(2):
                for d in range(2):
                    all_j[f, :, 4 * x + 2 * e + d, pl.ds(first, rows)] = gains[f, e, x, d] * factor

    pl.semaphore_wait(barrier, stn_count + 1)
    own = all_j.at[:, :, :, pl.ds(first, rows)]
    copies = [
        remote(own, own, send_sem.at[j - 1], recv_sem.at[j - 1], "stn", lax.rem(me + j, stn_count))
        for j in range(1, stn_count)
    ]
    sides = [
        remote(gains.at[pl.ds(chans - 2, 2)], before, side_send.at[0], side_recv.at[0], "chan", up),
        remote(gains.at[pl.ds(0, 2)], after, side_send.at[1], side_recv.at[1], "chan", down),
    ]
    for copy in copies + sides:
        copy.start()
    for copy in sides:
        copy.wait()

    last_chan = chans * chan_count - 2
    square = jnp.zeros((dirs, rows), jnp.float32)
    for e in range(2):
        for x in range(2):
            for d in range(2):
                line = (
                    [before[i, e, x, d] for i in range(2)]
                    + [gains[i, e, x, d] for i in range(chans)]
                    + [after[i, e, x, d] for i in range(2)]
                )
                second = []
                for i in range(chans + 2):
                    place = chan * chans - 1 + i
                    inside = ((place >= 1) & (place <= last_chan)).astype(jnp.float32)
                    second.append((line[i + 2] - 2.0 * line[i + 1] + line[i]) * inside)
                for i in range(chans):
                    smooth_out[i, e, x, d] = second[i] - 2.0 * second[i + 1] + second[i + 2]
                    square = square + second[i + 1] * second[i + 1]
    square_out[...] = jnp.sum(square.reshape(dirs // 8, 8, rows), axis=0)
    for copy in copies:
        copy.wait()


def finish_kernel(
    stn_count, chan_count, row_g, col_g, stats, smooth, square, factor,
    step_out, loss_out,
    landed, total, own_sums, buf_stn, buf_chan,
    send_sem, recv_sem, send_stn, recv_stn, send_chan, recv_chan,
):
    chans, _, rows = row_g.shape
    dirs = factor.shape[0]
    me, chan = lax.axis_index("stn"), lax.axis_index("chan")
    own_sums[...] = jnp.zeros_like(own_sums)
    for i in range(2):
        part = stats[0, i]
        for f in range(1, chans):
            part = part + stats[f, i]
        part = jnp.sum(part, axis=0, keepdims=True)
        line = part[:, :128]
        for at in range(128, part.shape[1], 128):
            line = line + part[:, at:at + 128]
        own_sums[i:i + 1, :] = line
    line = jnp.sum(square[...], axis=0, keepdims=True)
    part = line[:, :128]
    for at in range(128, line.shape[1], 128):
        part = part + line[:, at:at + 128]
    own_sums[2:3, :] = part
    buf_stn[me] = own_sums[...]

    meet((("stn", stn_count), ("chan", chan_count)))
    copies = []
    small = []
    for j in range(1, stn_count):
        peer = lax.rem(me + j, stn_count)
        small.append(remote(own_sums, buf_stn.at[me], send_stn.at[j - 1], recv_stn.at[j - 1], "stn", peer))
        copies.append(remote(
            col_g.at[:, :, pl.ds(pl.multiple_of(peer * rows, 128), rows)],
            landed.at[j - 1], send_sem.at[j - 1], recv_sem.at[j - 1], "stn", peer))
    for copy in small + copies:
        copy.start()
    for copy in small:
        copy.wait()
    sums = buf_stn[0]
    for i in range(1, stn_count):
        sums = sums + buf_stn[i]
    own_sums[...] = sums
    buf_chan[chan] = sums
    small = [
        remote(own_sums, buf_chan.at[chan], send_chan.at[j - 1], recv_chan.at[j - 1], "chan",
               lax.rem(chan + j, chan_count))
        for j in range(1, chan_count)
    ]
    for copy in small:
        copy.start()
    for f in range(chans):
        total[f] = row_g[f] + col_g[f, :, pl.ds(pl.multiple_of(me * rows, 128), rows)]
    for j, copy in enumerate(copies):
        copy.wait()
        for f in range(chans):
            total[f] = total[f] + landed[j, f]
    for copy in small:
        copy.wait()
    sums = buf_chan[0]
    for i in range(1, chan_count):
        sums = sums + buf_chan[i]
    sums = jnp.sum(sums, axis=1, keepdims=True)
    scale = (chans * chan_count * rows * stn_count) / sums[0:1]
    wide = jnp.broadcast_to(scale, (dirs, rows))
    gain = factor[...]
    for f in range(chans):
        curv = wide * gain * gain * total[f, dirs * 8:dirs * 9, :] + damping
        for e in range(2):
            for x in range(2):
                for d in range(2):
                    grad = total[f, pl.ds(4 * x + 2 * e + d, dirs, stride=8), :]
                    top = smooth_weight * smooth[f, e, x, d] - wide * gain * grad
                    step_out[f, e, x, d] = top / curv
    loss = (scale * sums[1:2] + smooth_weight * sums[2:3]) / (chans * chan_count * rows * stn_count)
    loss_out[0, 0] = jnp.sum(loss)


def on_device(gains, coherency, vis_data, flags, beam, group_of):
    chans, dirs, rows = gains.shape[0], gains.shape[4], gains.shape[5]
    stn, chan = lax.axis_size("stn"), lax.axis_size("chan")
    f4 = jnp.float32
    dma, vm = pltpu.SemaphoreType.DMA, pltpu.VMEM
    shape = jax.ShapeDtypeStruct
    all_j, factor, smooth, square = pl.pallas_call(
        functools.partial(gather_kernel, stn, chan),
        out_shape=[
            shape((chans, dirs, 8, rows * stn), f4),
            shape((dirs, rows), f4),
            shape(gains.shape, f4),
            shape((8, rows), f4),
        ],
        scratch_shapes=[
            vm((2,) + gains.shape[1:], f4),
            vm((2,) + gains.shape[1:], f4),
            dma((stn - 1,)), dma((stn - 1,)), dma((2,)), dma((2,)),
        ],
        compiler_params=pltpu.CompilerParams(collective_id=0, has_side_effects=True),
    )(gains, beam, group_of.reshape(1, -1))
    row_g, col_g, stats = device_terms(coherency, vis_data, flags, all_j)
    gain_step, loss = pl.pallas_call(
        functools.partial(finish_kernel, stn, chan),
        out_shape=[shape(gains.shape, f4), shape((1, 1), f4)],
        out_specs=[
            pl.BlockSpec(memory_space=pltpu.VMEM),
            pl.BlockSpec(memory_space=pltpu.SMEM),
        ],
        scratch_shapes=[
            vm((stn - 1,) + row_g.shape, f4),
            vm(row_g.shape, f4),
            vm((8, 128), f4),
            vm((stn, 8, 128), f4),
            vm((chan, 8, 128), f4),
            dma((stn - 1,)), dma((stn - 1,)), dma((stn - 1,)), dma((stn - 1,)),
            dma((chan - 1,)), dma((chan - 1,)),
        ],
        compiler_params=pltpu.CompilerParams(collective_id=1, has_side_effects=True),
    )(row_g, col_g, stats, smooth, square, factor)
    return (gain_step, loss.reshape(()))


def solution(mesh):
    in_specs = (
        P("chan", None, None, None, None, "stn"),
        P("chan", None, None, "stn", None),
        P("chan", None, None, None, "stn", None),
        P("chan", "stn", None),
        P(),
        P(),
    )
    out_specs = (P("chan", None, None, None, None, "stn"), P())
    return jax.shard_map(
        on_device, mesh=mesh, in_specs=in_specs, out_specs=out_specs, check_vma=False
    )
```
